32 devices in a mesh: pipe: 8 (over y, x, core), dp: 4 (over z).
Axes of the slice: x: 2, y: 2, z: 4, core: 2. Of those that a mesh axis runs over, the one named last changes fastest.
Arguments:
- inputs: bfloat16 [4, 128, 6144], P(None, 'dp'), may hold values from -6 to 6
- cotangent: bfloat16 [4, 128, 6144], P(None, 'dp'), may hold values from -6 to 6
- gains: float32 [8, 6144], P('pipe'), may hold values from 0.5 to 1.5
- w_value: bfloat16 [8, 6144, 128], P('pipe'), may hold values from -0.078125 to 0.078125
- w_out: bfloat16 [8, 128, 6144], P('pipe'), may hold values from -0.5 to 0.5
Outputs:
- grad_value: float32 [8, 6144, 128], P('pipe')
- grad_out: float32 [8, 128, 6144], P('pipe')
- grad_gain: float32 [8, 6144], P('pipe')
The draws below stay inside these ranges and needn't reach their ends.
All inputs are finite; a program needn't handle non-finite values.
Results may differ from the reference program's by a relative error of at most 0.02.
Values may be sent and summed in bfloat16 or wider, within the bound.
A program may use at most 64 MiB of HBM per device.

```python
import jax
import jax.numpy as jnp
from jax import lax

D = 6144
R = 128
M = 4
MB_TOK = 32
TOKENS = 128
SECTIONS = 8
N_PIPE = 8
N_DP = 4


def block_scale(key, dims, pieces, smallest, high):
    def one(axis_at, parts):
        steps = jax.random.uniform(jax.random.fold_in(jax.random.fold_in(key, 6), axis_at), (parts,), jnp.float32, smallest / len(pieces), high / len(pieces))
        return jnp.repeat(jnp.exp(steps), dims[axis_at] // parts).reshape((-1,) + (1,) * (len(dims) - axis_at - 1))

    factor_of = one(*pieces[0])
    for cut in pieces[1:]:
        factor_of = factor_of * one(*cut)
    return factor_of


def bell_draw(rng, extent, spread, reach, cuts=(), held_as=jnp.bfloat16):
    values = jax.random.normal(rng, extent, jnp.float32) * spread
    if len(cuts) > 0:
        values = block_scale(rng, extent, cuts, -0.22, 0.18) * values
    return jnp.clip(values, min=-reach, max=reach).astype(held_as)


def setup_inputs(seed: int = 0) -> dict:
    splits = jax.random.split(jax.random.key(seed), 6)
    return {
        "inputs": bell_draw(splits[0], (M, TOKENS, D), 1.0, 6.0, ((1, 4),)),
        "cotangent": bell_draw(splits[1], (M, TOKENS, D), 1.0, 6.0, ((1, 4),)),
        "gains": jnp.clip(1.0 + 0.1 * jax.random.normal(splits[2], (SECTIONS, D), jnp.float32), 0.5, 1.5),
        "w_value": bell_draw(splits[3], (SECTIONS, D, R), D ** -0.5, 0.078125, ((0, 8),)),
        "w_out": bell_draw(splits[4], (SECTIONS, R, D), R ** -0.5, 0.5, ((0, 8),)),
    }


epsilon = 1e-05

def normalize(floats):
    inv_rms = lax.rsqrt(lax.optimization_barrier(jnp.mean(floats * floats, axis=-1, keepdims=True)) + epsilon)
    return (floats * inv_rms, inv_rms)

def section_forward(hidden, gain_row, value_weight, out_weight):
    floats = hidden.astype(jnp.float32)
    normed, inv_rms = normalize(floats)
    mixed_rows = (normed * gain_row).astype(jnp.bfloat16)
    values = jnp.dot(mixed_rows, value_weight, preferred_element_type=jnp.float32).astype(jnp.bfloat16)
    branch = jnp.dot(values, out_weight, preferred_element_type=jnp.float32)
    return (floats + branch).astype(jnp.bfloat16)

def rounded_sum(partial_terms):
    low = lax.optimization_barrier(partial_terms.astype(jnp.bfloat16))
    return lax.optimization_barrier(jnp.sum(low.astype(jnp.float32), axis=0))

def reference(inputs, cotangent, gains, w_value, w_out):
    flat_rows = inputs.reshape(M * TOKENS, D)
    stashed = []
    for section_id in range(N_PIPE):
        stashed.append(flat_rows)
        flat_rows = section_forward(flat_rows, gains[section_id], w_value[section_id], w_out[section_id])
    upstream = cotangent.reshape(M * TOKENS, D)
    value_grads = []
    out_grads = []
    gain_grads = []
    for section_id in range(N_PIPE - 1, -1, -1):
        floats = stashed[section_id].astype(jnp.float32)
        normed, inv_rms = normalize(floats)
        mixed_rows = (normed * gains[section_id]).astype(jnp.bfloat16)
        values = jnp.dot(mixed_rows, w_value[section_id], preferred_element_type=jnp.float32).astype(jnp.bfloat16)
        upper = upstream.astype(jnp.float32)
        dvalues = jnp.dot(upstream, w_out[section_id].T, preferred_element_type=jnp.float32).astype(jnp.bfloat16)
        dmixed = jnp.dot(dvalues, w_value[section_id].T, preferred_element_type=jnp.float32)
        values_four = values.astype(jnp.float32).reshape(M, N_DP, MB_TOK, R)
        upper_four = upper.reshape(M, N_DP, MB_TOK, D)
        mixed_four = mixed_rows.astype(jnp.float32).reshape(M, N_DP, MB_TOK, D)
        dvalues_four = dvalues.astype(jnp.float32).reshape(M, N_DP, MB_TOK, R)
        out_grads.append(rounded_sum(jnp.einsum('mdtk,mdtj->dkj', values_four, upper_four)))
        value_grads.append(rounded_sum(jnp.einsum('mdtj,mdtk->djk', mixed_four, dvalues_four)))
        gain_terms = (dmixed * normed).reshape(M, N_DP, MB_TOK, D)
        gain_grads.append(rounded_sum(lax.optimization_barrier(jnp.sum(gain_terms, axis=(0, 2)))))
        dnormed = dmixed * gains[section_id]
        inner = lax.optimization_barrier(jnp.mean(dnormed * normed, axis=-1, keepdims=True))
        upstream = (upper + inv_rms * (dnormed - normed * inner)).astype(jnp.bfloat16)
    grad_value = jnp.stack(value_grads[::-1])
    grad_out = jnp.stack(out_grads[::-1])
    grad_gain = jnp.stack(gain_grads[::-1])
    return (grad_value, grad_out, grad_gain)
```

```python
import functools

import jax
import jax.numpy as jnp
from jax import lax
from jax.experimental import pallas as pl
from jax.experimental.pallas import tpu as pltpu
from jax.sharding import PartitionSpec as P

epsilon = 1e-05
MESH = pl.DeviceIdType.MESH
F32 = jnp.float32
BF16 = jnp.bfloat16
TAIL = 16


def dot(a, b, dims):
    return lax.dot_general(a, b, (dims, ((), ())), preferred_element_type=F32)


def split_rows(row):
    wide = jnp.broadcast_to(row, (TAIL, row.shape[-1]))
    high = wide.astype(BF16).astype(F32)
    at = lax.broadcasted_iota(jnp.int32, wide.shape, 0)
    return jnp.where(at < 8, high, wide - high).astype(BF16)


def joined_row(tail):
    tail = tail.astype(F32)
    return tail[0:1] + tail[8:9]


def as_column(row, lanes):
    return jnp.broadcast_to(row, (lanes, row.shape[-1])).T


def kernel(
    n_pipe, n_dp,
    gains, inputs, cotangent, w_value, w_out,
    gv_out, go_out, gg_out,
    wv_all, wo_all, ga_all, h0_all, cot_all, own_h, vq, xs, xbuf,
    h_all, g_all, g_own, acc_v, acc_o, acc_g, gs_v, gs_o, gs_g,
    w_send, w_recv, in_send, in_recv, x_send, x_recv,
    v_send, v_recv, d_send, d_recv, o_send, o_recv,
):
    me = lax.axis_index("pipe")
    z = lax.axis_index("dp")
    layers = n_pipe
    width = wv_all.shape[1]
    full = width * n_pipe
    rank = wv_all.shape[2]
    tokens = own_h.shape[1]

    def plane_peer(k):
        return lax.rem(me + k, n_pipe)

    def line_peer(k):
        return lax.rem(z + k, n_dp)

    barrier = pltpu.get_barrier_semaphore()
    for k in range(1, n_pipe):
        pl.semaphore_signal(barrier, inc=1, device_id=(plane_peer(k), z), device_id_type=MESH)
    for k in range(1, n_dp):
        pl.semaphore_signal(barrier, inc=1, device_id=(me, line_peer(k)), device_id_type=MESH)
    pl.semaphore_wait(barrier, n_pipe + n_dp - 2)

    def columns(owner):
        return pl.ds(pl.multiple_of(owner * width, width), width)

    def remote(src, dst, send, recv, to):
        return pltpu.make_async_remote_copy(
            src_ref=src, dst_ref=dst, send_sem=send, recv_sem=recv, device_id=to, device_id_type=MESH
        )

    def wait_local(dst, sem):
        pltpu.make_async_copy(dst, dst, sem).wait()

    pltpu.make_async_copy(inputs.at[:, :, columns(me)], h0_all.at[z], in_recv.at[0, 0]).start()
    pltpu.make_async_copy(cotangent.at[:, :, columns(me)], cot_all.at[z], in_recv.at[1, 0]).start()
    pltpu.make_async_copy(gains.at[:, columns(me)], ga_all.at[me], w_recv.at[0, me]).start()
    pltpu.make_async_copy(w_value.at[columns(me), :], wv_all.at[me], w_recv.at[1, me]).start()
    pltpu.make_async_copy(w_out.at[:, columns(me)], wo_all.at[me], w_recv.at[2, me]).start()

    def weight_copies(k):
        d = plane_peer(k)
        return (
            remote(gains.at[:, columns(d)], ga_all.at[me], w_send.at[0, k], w_recv.at[0, me], (d, z)),
            remote(w_value.at[columns(d), :], wv_all.at[me], w_send.at[1, k], w_recv.at[1, me], (d, z)),
            remote(w_out.at[:, columns(d)], wo_all.at[me], w_send.at[2, k], w_recv.at[2, me], (d, z)),
        )

    def input_copies(k):
        d = line_peer(k)
        return (
            remote(inputs.at[:, :, columns(me)], h0_all.at[z], in_send.at[0, k], in_recv.at[0, k], (me, d)),
            remote(cotangent.at[:, :, columns(me)], cot_all.at[z], in_send.at[1, k], in_recv.at[1, k], (me, d)),
        )

    def line_copies(buf, send, recv, s):
        return [
            remote(buf.at[s, z], buf.at[s, z], send.at[s, k], recv.at[s, k], (me, line_peer(k)))
            for k in range(1, n_dp)
        ]

    def exchange_copies(slot, rows):
        return [
            remote(
                xbuf.at[slot, 0, pl.ds(0, rows)], xbuf.at[slot, k, pl.ds(0, rows)],
                x_send.at[slot, k], x_recv.at[slot, k], (plane_peer(k), z),
            )
            for k in range(1, n_pipe)
        ]

    for k in range(1, n_pipe):
        for copy in weight_copies(k):
            copy.start()
    for k in range(1, n_dp):
        for copy in input_copies(k):
            copy.start()

    wait_local(h0_all.at[z], in_recv.at[0, 0])
    wait_local(cot_all.at[z], in_recv.at[1, 0])
    own_h[0] = h0_all[z].reshape(tokens, width)
    g_own[...] = cot_all[z].reshape(tokens, width).astype(F32)

    def forward(s, carry):
        slot = lax.rem(s, 2)
        wait_local(ga_all.at[s], w_recv.at[0, s])
        wait_local(wv_all.at[s], w_recv.at[1, s])
        floats = own_h[s].astype(F32)
        scaled = (floats * ga_all[s, 0:1, :]).astype(BF16)
        part = dot(scaled, wv_all[s], ((1,), (0,)))
        squares = dot(jnp.ones((8, width), BF16), (floats * floats).astype(BF16), ((1,), (1,)))
        xbuf[slot, 0, 0:tokens, :] = part.astype(BF16)
        xbuf[slot, 0, tokens:, :] = split_rows(squares[0:1])
        copies = exchange_copies(slot, tokens + TAIL)
        for copy in copies:
            copy.start()
        wait_local(wo_all.at[s], w_recv.at[2, s])
        row = joined_row(xbuf[slot, 0, tokens:, :])
        total = part
        for k, copy in enumerate(copies, 1):
            copy.wait_recv()
            total = total + xbuf[slot, k, 0:tokens, :].astype(F32)
            row = row + joined_row(xbuf[slot, k, tokens:, :])
        scale = lax.rsqrt(row * (1.0 / full) + epsilon)
        values = (total * as_column(scale, rank)).astype(BF16)
        vq[s, z, 0:tokens, :] = values
        vq[s, z, tokens:, :] = split_rows(scale)
        for copy in line_copies(vq, v_send, v_recv, s):
            copy.start()
        own_h[s + 1] = (floats + dot(values, wo_all[s], ((1,), (0,)))).astype(BF16)
        for copy in copies:
            copy.wait_send()
        return carry

    lax.fori_loop(0, layers, forward, 0)

    def fill_all():
        for k in range(1, n_dp):
            for copy in input_copies(k):
                copy.wait()

        def arrive(s, carry):
            for copy in line_copies(vq, v_send, v_recv, s):
                copy.wait()
            return carry

        lax.fori_loop(0, layers, arrive, 0)

        def replica(r, carry):
            g_all[r] = cot_all[r].reshape(tokens, width).astype(F32)
            h_all[r] = h0_all[r].reshape(tokens, width).astype(F32)

            def add(s, inner):
                h_all[r] += dot(vq[s, r, 0:tokens, :], wo_all[s], ((1,), (0,)))
                return inner

            lax.fori_loop(0, layers, add, 0)
            return carry

        lax.fori_loop(0, n_dp, replica, 0)

    def gradients(s):
        for copy in line_copies(xs, d_send, d_recv, s):
            copy.wait()
        acc_v[...] = jnp.zeros_like(acc_v)
        acc_o[...] = jnp.zeros_like(acc_o)
        acc_g[...] = jnp.zeros_like(acc_g)

        def replica(r, carry):
            gain = ga_all[s, 0:1, :]
            values = vq[s, r, 0:tokens, :]
            scale = as_column(joined_row(vq[s, r, tokens:, :]), rank)
            scaled_dv = xs[s, r]
            floats = h_all[r] - dot(values, wo_all[s], ((1,), (0,)))
            h_all[r] = floats
            upper = g_all[r]
            acc_o[...] += dot(values, upper.astype(BF16), ((0,), (0,)))
            acc_v[...] += dot((floats * gain).astype(BF16), scaled_dv, ((0,), (0,)))
            du = dot(scaled_dv, wv_all[s], ((1,), (1,)))
            acc_g[0:1, :] += jnp.sum(du * floats, axis=0, keepdims=True)
            weigh = jnp.sum(scaled_dv.astype(F32) * values.astype(F32) * scale, axis=1, keepdims=True)
            g_all[r] = upper + (du * gain - floats * (weigh * (1.0 / full)))
            return carry

        lax.fori_loop(0, n_dp, replica, 0)
        gs_v[s] = acc_v[...].astype(BF16)
        gs_o[s] = acc_o[...].astype(BF16)
        gs_g[s] = acc_g[...]

        @pl.when(s == me)
        def _():
            pltpu.make_async_copy(gs_v.at[s], gv_out.at[me], o_recv.at[0, me]).start()
            pltpu.make_async_copy(gs_o.at[s], go_out.at[:, columns(me)], o_recv.at[1, me]).start()
            pltpu.make_async_copy(gs_g.at[s], gg_out.at[me], o_recv.at[2, me]).start()

        @pl.when(s != me)
        def _():
            remote(gs_v.at[s], gv_out.at[me], o_send.at[0, s], o_recv.at[0, me], (s, z)).start()
            remote(gs_o.at[s], go_out.at[:, columns(me)], o_send.at[1, s], o_recv.at[1, me], (s, z)).start()
            remote(gs_g.at[s], gg_out.at[me], o_send.at[2, s], o_recv.at[2, me], (s, z)).start()

    def backward(i, carry):
        s = layers - 1 - i
        slot = lax.rem(layers + i, 2)
        upper = g_own[...]
        part = dot(upper.astype(BF16), wo_all[s], ((1,), (1,)))
        xbuf[slot, 0, 0:tokens, :] = part.astype(BF16)
        copies = exchange_copies(slot, tokens)
        for copy in copies:
            copy.start()

        @pl.when(i == 0)
        def _():
            fill_all()

        @pl.when(i > 0)
        def _():
            gradients(s + 1)

        total = part
        for k, copy in enumerate(copies, 1):
            copy.wait_recv()
            total = total + xbuf[slot, k, 0:tokens, :].astype(F32)
        scale = as_column(joined_row(vq[s, z, tokens:, :]), rank)
        scaled_dv = (total * scale).astype(BF16)
        xs[s, z] = scaled_dv
        for copy in line_copies(xs, d_send, d_recv, s):
            copy.start()
        values = vq[s, z, 0:tokens, :].astype(F32)
        weigh = jnp.sum(scaled_dv.astype(F32) * values * scale, axis=1, keepdims=True)
        du = dot(scaled_dv, wv_all[s], ((1,), (1,)))
        floats = own_h[s].astype(F32)
        g_own[...] = upper + (du * ga_all[s, 0:1, :] - floats * (weigh * (1.0 / full)))
        for copy in copies:
            copy.wait_send()
        return carry

    lax.fori_loop(0, layers, backward, 0)
    gradients(0)

    for k in range(1, n_pipe):
        for copy in weight_copies(k):
            copy.wait_send()

    def finish(s, carry):
        wait_local(gv_out.at[s], o_recv.at[0, s])
        wait_local(go_out.at[:, columns(s)], o_recv.at[1, s])
        wait_local(gg_out.at[s], o_recv.at[2, s])

        @pl.when(s != me)
        def _():
            remote(gs_v.at[s], gv_out.at[me], o_send.at[0, s], o_recv.at[0, me], (s, z)).wait_send()
            remote(gs_o.at[s], go_out.at[:, columns(me)], o_send.at[1, s], o_recv.at[1, me], (s, z)).wait_send()
            remote(gs_g.at[s], gg_out.at[me], o_send.at[2, s], o_recv.at[2, me], (s, z)).wait_send()

        return carry

    lax.fori_loop(0, n_pipe, finish, 0)


def per_device(n_pipe, n_dp, inputs, cotangent, gains, w_value, w_out):
    batches, rows, full = inputs.shape
    rank = w_value.shape[-1]
    width = full // n_pipe
    tokens = batches * rows
    layers = n_pipe
    any_spec = pl.BlockSpec(memory_space=pl.ANY)
    dma = pltpu.SemaphoreType.DMA
    gv, go, gg = pl.pallas_call(
        functools.partial(kernel, n_pipe, n_dp),
        out_shape=(
            jax.ShapeDtypeStruct((n_pipe, width, rank), BF16),
            jax.ShapeDtypeStruct((rank, full), BF16),
            jax.ShapeDtypeStruct((n_pipe, 8, width), F32),
        ),
        in_specs=[any_spec] * 5,
        out_specs=(any_spec,) * 3,
        scratch_shapes=[
            pltpu.VMEM((layers, width, rank), BF16),
            pltpu.VMEM((layers, rank, width), BF16),
            pltpu.VMEM((layers, 8, width), F32),
            pltpu.VMEM((n_dp, batches, rows, width), BF16),
            pltpu.VMEM((n_dp, batches, rows, width), BF16),
            pltpu.VMEM((layers + 1, tokens, width), BF16),
            pltpu.VMEM((layers, n_dp, tokens + TAIL, rank), BF16),
            pltpu.VMEM((layers, n_dp, tokens, rank), BF16),
            pltpu.VMEM((2, n_pipe, tokens + TAIL, rank), BF16),
            pltpu.VMEM((n_dp, tokens, width), F32),
            pltpu.VMEM((n_dp, tokens, width), F32),
            pltpu.VMEM((tokens, width), F32),
            pltpu.VMEM((width, rank), F32),
            pltpu.VMEM((rank, width), F32),
            pltpu.VMEM((8, width), F32),
            pltpu.VMEM((layers, width, rank), BF16),
            pltpu.VMEM((layers, rank, width), BF16),
            pltpu.VMEM((layers, 8, width), F32),
            dma((3, n_pipe)), dma((3, n_pipe)),
            dma((2, n_dp)), dma((2, n_dp)),
            dma((2, n_pipe)), dma((2, n_pipe)),
            dma((layers, n_dp)), dma((layers, n_dp)),
            dma((layers, n_dp)), dma((layers, n_dp)),
            dma((3, n_pipe)), dma((3, n_pipe)),
        ],
        compiler_params=pltpu.CompilerParams(
            collective_id=0, has_side_effects=True, vmem_limit_bytes=56 * 1024 * 1024
        ),
        cost_estimate=pl.CostEstimate(
            flops=40 * n_dp * tokens * full * rank, bytes_accessed=16 * full * rank, transcendentals=0
        ),
    )(jnp.broadcast_to(gains, (8, full)), inputs, cotangent, w_value[0], w_out[0])
    return (
        gv.reshape(1, full, rank).astype(F32),
        go[None].astype(F32),
        gg[:, 0, :].reshape(1, full),
    )


def solution(mesh):
    placed = (
        P(None, "dp", None),
        P(None, "dp", None),
        P("pipe", None),
        P("pipe", None, None),
        P("pipe", None, None),
    )
    return jax.shard_map(
        functools.partial(per_device, mesh.shape["pipe"], mesh.shape["dp"]),
        mesh=mesh,
        in_specs=placed,
        out_specs=(P("pipe", None, None), P("pipe", None, None), P("pipe", None)),
        check_vma=False,
    )
```

```python
import functools

import jax
import jax.numpy as jnp
from jax import lax
from jax.experimental import pallas as pl
from jax.experimental.pallas import tpu as pltpu
from jax.sharding import PartitionSpec as P

epsilon = 1e-05
MESH = pl.DeviceIdType.MESH
F32 = jnp.float32
BF16 = jnp.bfloat16
TAIL = 16


def dot(a, b, dims):
    return lax.dot_general(a, b, (dims, ((), ())), preferred_element_type=F32)


def split_rows(row):
    wide = jnp.broadcast_to(row, (TAIL, row.shape[-1]))
    high = wide.astype(BF16).astype(F32)
    at = lax.broadcasted_iota(jnp.int32, wide.shape, 0)
    return jnp.where(at < 8, high, wide - high).astype(BF16)


def joined_row(tail):
    tail = tail.astype(F32)
    return tail[0:1] + tail[8:9]


def as_column(row, lanes):
    return jnp.broadcast_to(row, (lanes, row.shape[-1])).T


def kernel(
    n_pipe, n_dp,
    gains, inputs, cotangent, w_value, w_out,
    gv_out, go_out, gg_out,
    wv_all, wo_all, ga_all, h0_all, cot_all, own_h, vq, xs, xbuf,
    h_all, g_all, g_own, acc_v, acc_o, acc_g, gs_v, gs_o, gs_g,
    w_send, w_recv, in_send, in_recv, x_send, x_recv,
    v_send, v_recv, d_send, d_recv, o_send, o_recv,
):
    me = lax.axis_index("pipe")
    z = lax.axis_index("dp")
    layers = n_pipe
    width = wv_all.shape[1]
    full = width * n_pipe
    rank = wv_all.shape[2]
    tokens = own_h.shape[1]

    def plane_peer(k):
        return lax.rem(me + k, n_pipe)

    def line_peer(k):
        return lax.rem(z + k, n_dp)

    barrier = pltpu.get_barrier_semaphore()
    for k in range(1, n_pipe):
        pl.semaphore_signal(barrier, inc=1, device_id=(plane_peer(k), z), device_id_type=MESH)
    for k in range(1, n_dp):
        pl.semaphore_signal(barrier, inc=1, device_id=(me, line_peer(k)), device_id_type=MESH)
    pl.semaphore_wait(barrier, n_pipe + n_dp - 2)

    def columns(owner):
        return pl.ds(pl.multiple_of(owner * width, width), width)

    def remote(src, dst, send, recv, to):
        return pltpu.make_async_remote_copy(
            src_ref=src, dst_ref=dst, send_sem=send, recv_sem=recv, device_id=to, device_id_type=MESH
        )

    def wait_local(dst, sem):
        pltpu.make_async_copy(dst, dst, sem).wait()

    pltpu.make_async_copy(inputs.at[:, :, columns(me)], h0_all.at[z], in_recv.at[0, 0]).start()
    pltpu.make_async_copy(cotangent.at[:, :, columns(me)], cot_all.at[z], in_recv.at[1, 0]).start()
    pltpu.make_async_copy(gains.at[:, columns(me)], ga_all.at[me], w_recv.at[0, me]).start()
    pltpu.make_async_copy(w_value.at[columns(me), :], wv_all.at[me], w_recv.at[1, me]).start()
    pltpu.make_async_copy(w_out.at[:, columns(me)], wo_all.at[me], w_recv.at[2, me]).start()

    def weight_copies(k):
        d = plane_peer(k)
        return (
            remote(gains.at[:, columns(d)], ga_all.at[me], w_send.at[0, k], w_recv.at[0, me], (d, z)),
            remote(w_value.at[columns(d), :], wv_all.at[me], w_send.at[1, k], w_recv.at[1, me], (d, z)),
            remote(w_out.at[:, columns(d)], wo_all.at[me], w_send.at[2, k], w_recv.at[2, me], (d, z)),
        )

    def input_copies(k):
        d = line_peer(k)
        return (
            remote(inputs.at[:, :, columns(me)], h0_all.at[z], in_send.at[0, k], in_recv.at[0, k], (me, d)),
            remote(cotangent.at[:, :, columns(me)], cot_all.at[z], in_send.at[1, k], in_recv.at[1, k], (me, d)),
        )

    def line_copies(buf, send, recv, s):
        return [
            remote(buf.at[s, z], buf.at[s, z], send.at[s, k], recv.at[s, k], (me, line_peer(k)))
            for k in range(1, n_dp)
        ]

    def exchange_copies(slot, rows):
        return [
            remote(
                xbuf.at[slot, 0, pl.ds(0, rows)], xbuf.at[slot, k, pl.ds(0, rows)],
                x_send.at[slot, k], x_recv.at[slot, k], (plane_peer(k), z),
            )
            for k in range(1, n_pipe)
        ]

    for k in range(1, n_pipe):
        for copy in weight_copies(k):
            copy.start()
    for k in range(1, n_dp):
        for copy in input_copies(k):
            copy.start()

    wait_local(h0_all.at[z], in_recv.at[0, 0])
    wait_local(cot_all.at[z], in_recv.at[1, 0])
    own_h[0] = h0_all[z].reshape(tokens, width)
    g_own[...] = cot_all[z].reshape(tokens, width).astype(F32)

    def forward(s, carry):
        slot = lax.rem(s, 2)
        wait_local(ga_all.at[s], w_recv.at[0, s])
        wait_local(wv_all.at[s], w_recv.at[1, s])
        floats = own_h[s].astype(F32)
        scaled = (floats * ga_all[s, 0:1, :]).astype(BF16)
        part = dot(scaled, wv_all[s], ((1,), (0,)))
        squares = dot(jnp.ones((8, width), BF16), (floats * floats).astype(BF16), ((1,), (1,)))
        xbuf[slot, 0, 0:tokens, :] = part.astype(BF16)
        xbuf[slot, 0, tokens:, :] = split_rows(squares[0:1])
        copies = exchange_copies(slot, tokens + TAIL)
        for copy in copies:
            copy.start()
        wait_local(wo_all.at[s], w_recv.at[2, s])
        row = joined_row(xbuf[slot, 0, tokens:, :])
        total = part
        for k, copy in enumerate(copies, 1):
            copy.wait_recv()
            total = total + xbuf[slot, k, 0:tokens, :].astype(F32)
            row = row + joined_row(xbuf[slot, k, tokens:, :])
        scale = lax.rsqrt(row * (1.0 / full) + epsilon)
        values = (total * as_column(scale, rank)).astype(BF16)
        vq[s, z, 0:tokens, :] = values
        vq[s, z, tokens:, :] = split_rows(scale)
        for copy in line_copies(vq, v_send, v_recv, s):
            copy.start()
        own_h[s + 1] = (floats + dot(values, wo_all[s], ((1,), (0,)))).astype(BF16)
        for copy in copies:
            copy.wait_send()
        return carry

    lax.fori_loop(0, layers, forward, 0)

    def fill_all():
        for k in range(1, n_dp):
            for copy in input_copies(k):
                copy.wait()

        def arrive(s, carry):
            for copy in line_copies(vq, v_send, v_recv, s):
                copy.wait()
            return carry

        lax.fori_loop(0, layers, arrive, 0)

        def replica(r, carry):
            g_all[r] = cot_all[r].reshape(tokens, width).astype(F32)
            h_all[r] = h0_all[r].reshape(tokens, width).astype(F32)

            def add(s, inner):
                h_all[r] += dot(vq[s, r, 0:tokens, :], wo_all[s], ((1,), (0,)))
                return inner

            lax.fori_loop(0, layers, add, 0)
            return carry

        lax.fori_loop(0, n_dp, replica, 0)

    def gradients(s):
        for copy in line_copies(xs, d_send, d_recv, s):
            copy.wait()
        acc_v[...] = jnp.zeros_like(acc_v)
        acc_o[...] = jnp.zeros_like(acc_o)
        acc_g[...] = jnp.zeros_like(acc_g)

        def replica(r, carry):
            gain = ga_all[s, 0:1, :]
            values = vq[s, r, 0:tokens, :]
            scale = as_column(joined_row(vq[s, r, tokens:, :]), rank)
            scaled_dv = xs[s, r]
            floats = h_all[r] - dot(values, wo_all[s], ((1,), (0,)))
            h_all[r] = floats
            upper = g_all[r]
            acc_o[...] += dot(values, upper.astype(BF16), ((0,), (0,)))
            acc_v[...] += dot((floats * gain).astype(BF16), scaled_dv, ((0,), (0,)))
            du = dot(scaled_dv, wv_all[s], ((1,), (1,)))
            acc_g[0:1, :] += jnp.sum(du * floats, axis=0, keepdims=True)
            weigh = jnp.sum(scaled_dv.astype(F32) * values.astype(F32) * scale, axis=1, keepdims=True)
            g_all[r] = upper + (du * gain - floats * (weigh * (1.0 / full)))
            return carry

        lax.fori_loop(0, n_dp, replica, 0)
        gs_v[s] = acc_v[...].astype(BF16)
        gs_o[s] = acc_o[...].astype(BF16)
        gs_g[s] = acc_g[...]

    def send_out(s):
        @pl.when(s == me)
        def _():
            pltpu.make_async_copy(gs_v.at[s], gv_out.at[me], o_recv.at[0, me]).start()
            pltpu.make_async_copy(gs_o.at[s], go_out.at[:, columns(me)], o_recv.at[1, me]).start()
            pltpu.make_async_copy(gs_g.at[s], gg_out.at[me], o_recv.at[2, me]).start()

        @pl.when(s != me)
        def _():
            remote(gs_v.at[s], gv_out.at[me], o_send.at[0, s], o_recv.at[0, me], (s, z)).start()
            remote(gs_o.at[s], go_out.at[:, columns(me)], o_send.at[1, s], o_recv.at[1, me], (s, z)).start()
            remote(gs_g.at[s], gg_out.at[me], o_send.at[2, s], o_recv.at[2, me], (s, z)).start()

    def backward(i, carry):
        s = layers - 1 - i
        slot = lax.rem(layers + i, 2)
        upper = g_own[...]
        part = dot(upper.astype(BF16), wo_all[s], ((1,), (1,)))
        xbuf[slot, 0, 0:tokens, :] = part.astype(BF16)
        copies = exchange_copies(slot, tokens)
        for copy in copies:
            copy.start()

        @pl.when(i == 0)
        def _():
            fill_all()

        @pl.when(i > 0)
        def _():
            gradients(s + 1)

        total = part
        for k, copy in enumerate(copies, 1):
            copy.wait_recv()
            total = total + xbuf[slot, k, 0:tokens, :].astype(F32)
        scale = as_column(joined_row(vq[s, z, tokens:, :]), rank)
        scaled_dv = (total * scale).astype(BF16)
        xs[s, z] = scaled_dv
        for copy in line_copies(xs, d_send, d_recv, s):
            copy.start()
        values = vq[s, z, 0:tokens, :].astype(F32)
        weigh = jnp.sum(scaled_dv.astype(F32) * values * scale, axis=1, keepdims=True)
        du = dot(scaled_dv, wv_all[s], ((1,), (1,)))
        floats = own_h[s].astype(F32)
        g_own[...] = upper + (du * ga_all[s, 0:1, :] - floats * (weigh * (1.0 / full)))
        for copy in copies:
            copy.wait_send()
        return carry

    lax.fori_loop(0, layers, backward, 0)
    gradients(0)

    def send_all(k, carry):
        send_out(lax.rem(me + k, n_pipe))
        return carry

    lax.fori_loop(0, n_pipe, send_all, 0)

    for k in range(1, n_pipe):
        for copy in weight_copies(k):
            copy.wait_send()

    def finish(s, carry):
        wait_local(gv_out.at[s], o_recv.at[0, s])
        wait_local(go_out.at[:, columns(s)], o_recv.at[1, s])
        wait_local(gg_out.at[s], o_recv.at[2, s])

        @pl.when(s != me)
        def _():
            remote(gs_v.at[s], gv_out.at[me], o_send.at[0, s], o_recv.at[0, me], (s, z)).wait_send()
            remote(gs_o.at[s], go_out.at[:, columns(me)], o_send.at[1, s], o_recv.at[1, me], (s, z)).wait_send()
            remote(gs_g.at[s], gg_out.at[me], o_send.at[2, s], o_recv.at[2, me], (s, z)).wait_send()

        return carry

    lax.fori_loop(0, n_pipe, finish, 0)


def per_device(n_pipe, n_dp, inputs, cotangent, gains, w_value, w_out):
    batches, rows, full = inputs.shape
    rank = w_value.shape[-1]
    width = full // n_pipe
    tokens = batches * rows
    layers = n_pipe
    any_spec = pl.BlockSpec(memory_space=pl.ANY)
    dma = pltpu.SemaphoreType.DMA
    gv, go, gg = pl.pallas_call(
        functools.partial(kernel, n_pipe, n_dp),
        out_shape=(
            jax.ShapeDtypeStruct((n_pipe, width, rank), BF16),
            jax.ShapeDtypeStruct((rank, full), BF16),
            jax.ShapeDtypeStruct((n_pipe, 8, width), F32),
        ),
        in_specs=[any_spec] * 5,
        out_specs=(any_spec,) * 3,
        scratch_shapes=[
            pltpu.VMEM((layers, width, rank), BF16),
            pltpu.VMEM((layers, rank, width), BF16),
            pltpu.VMEM((layers, 8, width), F32),
            pltpu.VMEM((n_dp, batches, rows, width), BF16),
            pltpu.VMEM((n_dp, batches, rows, width), BF16),
            pltpu.VMEM((layers + 1, tokens, width), BF16),
            pltpu.VMEM((layers, n_dp, tokens + TAIL, rank), BF16),
            pltpu.VMEM((layers, n_dp, tokens, rank), BF16),
            pltpu.VMEM((2, n_pipe, tokens + TAIL, rank), BF16),
            pltpu.VMEM((n_dp, tokens, width), F32),
            pltpu.VMEM((n_dp, tokens, width), F32),
            pltpu.VMEM((tokens, width), F32),
            pltpu.VMEM((width, rank), F32),
            pltpu.VMEM((rank, width), F32),
            pltpu.VMEM((8, width), F32),
            pltpu.VMEM((layers, width, rank), BF16),
            pltpu.VMEM((layers, rank, width), BF16),
            pltpu.VMEM((layers, 8, width), F32),
            dma((3, n_pipe)), dma((3, n_pipe)),
            dma((2, n_dp)), dma((2, n_dp)),
            dma((2, n_pipe)), dma((2, n_pipe)),
            dma((layers, n_dp)), dma((layers, n_dp)),
            dma((layers, n_dp)), dma((layers, n_dp)),
            dma((3, n_pipe)), dma((3, n_pipe)),
        ],
        compiler_params=pltpu.CompilerParams(
            collective_id=0, has_side_effects=True, vmem_limit_bytes=56 * 1024 * 1024
        ),
        cost_estimate=pl.CostEstimate(
            flops=40 * n_dp * tokens * full * rank, bytes_accessed=16 * full * rank, transcendentals=0
        ),
    )(jnp.broadcast_to(gains, (8, full)), inputs, cotangent, w_value[0], w_out[0])
    return (
        gv.reshape(1, full, rank).astype(F32),
        go[None].astype(F32),
        gg[:, 0, :].reshape(1, full),
    )


def solution(mesh):
    placed = (
        P(None, "dp", None),
        P(None, "dp", None),
        P("pipe", None),
        P("pipe", None, None),
        P("pipe", None, None),
    )
    return jax.shard_map(
        functools.partial(per_device, mesh.shape["pipe"], mesh.shape["dp"]),
        mesh=mesh,
        in_specs=placed,
        out_specs=(P("pipe", None, None), P("pipe", None, None), P("pipe", None)),
        check_vma=False,
    )
```

```python
import functools

import jax
import jax.numpy as jnp
from jax import lax
from jax.experimental import pallas as pl
from jax.experimental.pallas import tpu as pltpu
from jax.sharding import PartitionSpec as P

epsilon = 1e-05
MESH = pl.DeviceIdType.MESH
F32 = jnp.float32
BF16 = jnp.bfloat16
TAIL = 16


def dot(a, b, dims):
    return lax.dot_general(a, b, (dims, ((), ())), preferred_element_type=F32)


def split_rows(row):
    wide = jnp.broadcast_to(row, (TAIL, row.shape[-1]))
    high = wide.astype(BF16).astype(F32)
    at = lax.broadcasted_iota(jnp.int32, wide.shape, 0)
    return jnp.where(at < 8, high, wide - high).astype(BF16)


def joined_row(tail):
    tail = tail.astype(F32)
    return tail[0:1] + tail[8:9]


def as_column(row, lanes):
    return jnp.broadcast_to(row, (lanes, row.shape[-1])).T


def kernel(
    n_pipe, n_dp,
    gains, inputs, cotangent, w_value, w_out,
    gv_out, go_out, gg_out,
    wv_all, wo_all, ga_all, h0_all, cot_all, own_h, vq, xs, xbuf,
    h_all, g_all, g_own, acc_v, acc_o, acc_g, gs_v, gs_o, gs_g,
    w_send, w_recv, in_send, in_recv, x_send, x_recv,
    v_send, v_recv, d_send, d_recv, o_send, o_recv,
):
    me = lax.axis_index("pipe")
    z = lax.axis_index("dp")
    layers = n_pipe
    width = wv_all.shape[1]
    full = width * n_pipe
    rank = wv_all.shape[2]
    tokens = own_h.shape[1]

    def plane_peer(k):
        return lax.rem(me + k, n_pipe)

    def line_peer(k):
        return lax.rem(z + k, n_dp)

    barrier = pltpu.get_barrier_semaphore()
    for k in range(1, n_pipe):
        pl.semaphore_signal(barrier, inc=1, device_id=(plane_peer(k), z), device_id_type=MESH)
    for k in range(1, n_dp):
        pl.semaphore_signal(barrier, inc=1, device_id=(me, line_peer(k)), device_id_type=MESH)
    pl.semaphore_wait(barrier, n_pipe + n_dp - 2)

    def columns(owner):
        return pl.ds(pl.multiple_of(owner * width, width), width)

    def remote(src, dst, send, recv, to):
        return pltpu.make_async_remote_copy(
            src_ref=src, dst_ref=dst, send_sem=send, recv_sem=recv, device_id=to, device_id_type=MESH
        )

    def wait_local(dst, sem):
        pltpu.make_async_copy(dst, dst, sem).wait()

    pltpu.make_async_copy(inputs.at[:, :, columns(me)], h0_all.at[z], in_recv.at[0, 0]).start()
    pltpu.make_async_copy(cotangent.at[:, :, columns(me)], cot_all.at[z], in_recv.at[1, 0]).start()
    pltpu.make_async_copy(gains.at[:, columns(me)], ga_all.at[me], w_recv.at[0, me]).start()
    pltpu.make_async_copy(w_value.at[columns(me), :], wv_all.at[me], w_recv.at[1, me]).start()
    pltpu.make_async_copy(w_out.at[:, columns(me)], wo_all.at[me], w_recv.at[2, me]).start()

    def weight_copies(k):
        d = plane_peer(k)
        return (
            remote(gains.at[:, columns(d)], ga_all.at[me], w_send.at[0, k], w_recv.at[0, me], (d, z)),
            remote(w_value.at[columns(d), :], wv_all.at[me], w_send.at[1, k], w_recv.at[1, me], (d, z)),
            remote(w_out.at[:, columns(d)], wo_all.at[me], w_send.at[2, k], w_recv.at[2, me], (d, z)),
        )

    def input_copies(k):
        d = line_peer(k)
        return (
            remote(inputs.at[:, :, columns(me)], h0_all.at[z], in_send.at[0, k], in_recv.at[0, k], (me, d)),
            remote(cotangent.at[:, :, columns(me)], cot_all.at[z], in_send.at[1, k], in_recv.at[1, k], (me, d)),
        )

    def line_copies(buf, send, recv, s):
        return [
            remote(buf.at[s, z], buf.at[s, z], send.at[s, k], recv.at[s, k], (me, line_peer(k)))
            for k in range(1, n_dp)
        ]

    def exchange_copies(slot, rows):
        return [
            remote(
                xbuf.at[slot, 0, pl.ds(0, rows)], xbuf.at[slot, k, pl.ds(0, rows)],
                x_send.at[slot, k], x_recv.at[slot, k], (plane_peer(k), z),
            )
            for k in range(1, n_pipe)
        ]

    for k in range(1, n_pipe):
        for copy in weight_copies(k):
            copy.start()
    for k in range(1, n_dp):
        for copy in input_copies(k):
            copy.start()

    wait_local(h0_all.at[z], in_recv.at[0, 0])
    wait_local(cot_all.at[z], in_recv.at[1, 0])
    own_h[0] = h0_all[z].reshape(tokens, width)
    g_own[...] = cot_all[z].reshape(tokens, width).astype(F32)

    def forward(s, carry):
        slot = lax.rem(s, 2)
        wait_local(ga_all.at[s], w_recv.at[0, s])
        wait_local(wv_all.at[s], w_recv.at[1, s])
        floats = own_h[s].astype(F32)
        scaled = (floats * ga_all[s, 0:1, :]).astype(BF16)
        part = dot(scaled, wv_all[s], ((1,), (0,)))
        squares = dot(jnp.ones((8, width), BF16), (floats * floats).astype(BF16), ((1,), (1,)))
        xbuf[slot, 0, 0:tokens, :] = part.astype(BF16)
        xbuf[slot, 0, tokens:, :] = split_rows(squares[0:1])
        copies = exchange_copies(slot, tokens + TAIL)
        for copy in copies:
            copy.start()
        wait_local(wo_all.at[s], w_recv.at[2, s])
        row = joined_row(xbuf[slot, 0, tokens:, :])
        total = part
        for k, copy in enumerate(copies, 1):
            copy.wait_recv()
            total = total + xbuf[slot, k, 0:tokens, :].astype(F32)
            row = row + joined_row(xbuf[slot, k, tokens:, :])
        scale = lax.rsqrt(row * (1.0 / full) + epsilon)
        values = (total * as_column(scale, rank)).astype(BF16)
        vq[s, z, 0:tokens, :] = values
        vq[s, z, tokens:, :] = split_rows(scale)
        for copy in line_copies(vq, v_send, v_recv, s):
            copy.start()
        own_h[s + 1] = (floats + dot(values, wo_all[s], ((1,), (0,)))).astype(BF16)
        for copy in copies:
            copy.wait_send()
        return carry

    lax.fori_loop(0, layers, forward, 0)

    def fill_all():
        for k in range(1, n_dp):
            for copy in input_copies(k):
                copy.wait()

        def arrive(s, carry):
            for copy in line_copies(vq, v_send, v_recv, s):
                copy.wait()
            return carry

        lax.fori_loop(0, layers, arrive, 0)

        def replica(r, carry):
            g_all[r] = cot_all[r].reshape(tokens, width).astype(F32)
            h_all[r] = h0_all[r].reshape(tokens, width).astype(F32)

            def add(s, inner):
                h_all[r] += dot(vq[s, r, 0:tokens, :], wo_all[s], ((1,), (0,)))
                return inner

            lax.fori_loop(0, layers, add, 0)
            return carry

        lax.fori_loop(0, n_dp, replica, 0)

    def gradients(s):
        for copy in line_copies(xs, d_send, d_recv, s):
            copy.wait()
        acc_v[...] = jnp.zeros_like(acc_v)
        acc_o[...] = jnp.zeros_like(acc_o)
        acc_g[...] = jnp.zeros_like(acc_g)

        def replica(r, carry):
            gain = ga_all[s, 0:1, :]
            values = vq[s, r, 0:tokens, :]
            scale = as_column(joined_row(vq[s, r, tokens:, :]), rank)
            scaled_dv = xs[s, r]
            floats = h_all[r] - dot(values, wo_all[s], ((1,), (0,)))
            h_all[r] = floats
            upper = g_all[r]
            acc_o[...] += dot(values, upper.astype(BF16), ((0,), (0,)))
            acc_v[...] += dot((floats * gain).astype(BF16), scaled_dv, ((0,), (0,)))
            du = dot(scaled_dv, wv_all[s], ((1,), (1,)))
            acc_g[0:1, :] += jnp.sum(du * floats, axis=0, keepdims=True)
            weigh = jnp.sum(scaled_dv.astype(F32) * values.astype(F32) * scale, axis=1, keepdims=True)
            g_all[r] = upper + (du * gain - floats * (weigh * (1.0 / full)))
            return carry

        lax.fori_loop(0, n_dp, replica, 0)
        gs_v[s] = acc_v[...].astype(BF16)
        gs_o[s] = acc_o[...].astype(BF16)
        gs_g[s] = acc_g[...]

    def send_out(s):
        @pl.when(s == me)
        def _():
            pltpu.make_async_copy(gs_v.at[s], gv_out.at[me], o_recv.at[0, me]).start()
            pltpu.make_async_copy(gs_o.at[s], go_out.at[:, columns(me)], o_recv.at[1, me]).start()
            pltpu.make_async_copy(gs_g.at[s], gg_out.at[me], o_recv.at[2, me]).start()

        @pl.when(s != me)
        def _():
            remote(gs_v.at[s], gv_out.at[me], o_send.at[0, s], o_recv.at[0, me], (s, z)).start()
            remote(gs_o.at[s], go_out.at[:, columns(me)], o_send.at[1, s], o_recv.at[1, me], (s, z)).start()
            remote(gs_g.at[s], gg_out.at[me], o_send.at[2, s], o_recv.at[2, me], (s, z)).start()

    def backward(i, carry):
        s = layers - 1 - i
        slot = lax.rem(layers + i, 2)
        upper = g_own[...]
        part = dot(upper.astype(BF16), wo_all[s], ((1,), (1,)))
        xbuf[slot, 0, 0:tokens, :] = part.astype(BF16)
        copies = exchange_copies(slot, tokens)
        for copy in copies:
            copy.start()

        @pl.when(i == 0)
        def _():
            fill_all()

        @pl.when(i > 0)
        def _():
            gradients(s + 1)

        total = part
        for k, copy in enumerate(copies, 1):
            copy.wait_recv()
            total = total + xbuf[slot, k, 0:tokens, :].astype(F32)
        scale = as_column(joined_row(vq[s, z, tokens:, :]), rank)
        scaled_dv = (total * scale).astype(BF16)
        xs[s, z] = scaled_dv
        for copy in line_copies(xs, d_send, d_recv, s):
            copy.start()
        values = vq[s, z, 0:tokens, :].astype(F32)
        weigh = jnp.sum(scaled_dv.astype(F32) * values * scale, axis=1, keepdims=True)
        du = dot(scaled_dv, wv_all[s], ((1,), (1,)))
        floats = own_h[s].astype(F32)
        g_own[...] = upper + (du * ga_all[s, 0:1, :] - floats * (weigh * (1.0 / full)))
        for copy in copies:
            copy.wait_send()
        return carry

    lax.fori_loop(0, layers, backward, 0)
    gradients(0)

    def send_all(k, carry):
        send_out(lax.rem(me + k, n_pipe))
        return carry

    lax.fori_loop(0, n_pipe, send_all, 0)

    for k in range(1, n_pipe):
        for copy in weight_copies(k):
            copy.wait_send()

    def finish(s, carry):
        wait_local(gv_out.at[s], o_recv.at[0, s])
        wait_local(go_out.at[:, columns(s)], o_recv.at[1, s])
        wait_local(gg_out.at[s], o_recv.at[2, s])

        @pl.when(s != me)
        def _():
            remote(gs_v.at[s], gv_out.at[me], o_send.at[0, s], o_recv.at[0, me], (s, z)).wait_send()
            remote(gs_o.at[s], go_out.at[:, columns(me)], o_send.at[1, s], o_recv.at[1, me], (s, z)).wait_send()
            remote(gs_g.at[s], gg_out.at[me], o_send.at[2, s], o_recv.at[2, me], (s, z)).wait_send()

        return carry

    lax.fori_loop(0, n_pipe, finish, 0)


def per_device(n_pipe, n_dp, inputs, cotangent, gains, w_value, w_out):
    batches, rows, full = inputs.shape
    rank = w_value.shape[-1]
    width = full // n_pipe
    tokens = batches * rows
    layers = n_pipe
    any_spec = pl.BlockSpec(memory_space=pl.ANY)
    dma = pltpu.SemaphoreType.DMA
    gv, go, gg = pl.pallas_call(
        functools.partial(kernel, n_pipe, n_dp),
        out_shape=(
            jax.ShapeDtypeStruct((n_pipe, width, rank), BF16),
            jax.ShapeDtypeStruct((rank, full), BF16),
            jax.ShapeDtypeStruct((n_pipe, 1, width), F32),
        ),
        in_specs=[any_spec] * 5,
        out_specs=(any_spec,) * 3,
        scratch_shapes=[
            pltpu.VMEM((layers, width, rank), BF16),
            pltpu.VMEM((layers, rank, width), BF16),
            pltpu.VMEM((layers, 1, width), F32),
            pltpu.VMEM((n_dp, batches, rows, width), BF16),
            pltpu.VMEM((n_dp, batches, rows, width), BF16),
            pltpu.VMEM((layers + 1, tokens, width), BF16),
            pltpu.VMEM((layers, n_dp, tokens + TAIL, rank), BF16),
            pltpu.VMEM((layers, n_dp, tokens, rank), BF16),
            pltpu.VMEM((2, n_pipe, tokens + TAIL, rank), BF16),
            pltpu.VMEM((n_dp, tokens, width), F32),
            pltpu.VMEM((n_dp, tokens, width), F32),
            pltpu.VMEM((tokens, width), F32),
            pltpu.VMEM((width, rank), F32),
            pltpu.VMEM((rank, width), F32),
            pltpu.VMEM((1, width), F32),
            pltpu.VMEM((layers, width, rank), BF16),
            pltpu.VMEM((layers, rank, width), BF16),
            pltpu.VMEM((layers, 1, width), F32),
            dma((3, n_pipe)), dma((3, n_pipe)),
            dma((2, n_dp)), dma((2, n_dp)),
            dma((2, n_pipe)), dma((2, n_pipe)),
            dma((layers, n_dp)), dma((layers, n_dp)),
            dma((layers, n_dp)), dma((layers, n_dp)),
            dma((3, n_pipe)), dma((3, n_pipe)),
        ],
        compiler_params=pltpu.CompilerParams(
            collective_id=0, has_side_effects=True, vmem_limit_bytes=56 * 1024 * 1024
        ),
        cost_estimate=pl.CostEstimate(
            flops=40 * n_dp * tokens * full * rank, bytes_accessed=16 * full * rank, transcendentals=0
        ),
    )(gains, inputs, cotangent, w_value[0], w_out[0])
    return (
        gv.reshape(1, full, rank).astype(F32),
        go[None].astype(F32),
        gg.reshape(1, full),
    )


def solution(mesh):
    placed = (
        P(None, "dp", None),
        P(None, "dp", None),
        P("pipe", None),
        P("pipe", None, None),
        P("pipe", None, None),
    )
    return jax.shard_map(
        functools.partial(per_device, mesh.shape["pipe"], mesh.shape["dp"]),
        mesh=mesh,
        in_specs=placed,
        out_specs=(P("pipe", None, None), P("pipe", None, None), P("pipe", None)),
        check_vma=False,
    )
```

```python
import functools

import jax
import jax.numpy as jnp
from jax import lax
from jax.experimental import pallas as pl
from jax.experimental.pallas import tpu as pltpu
from jax.sharding import PartitionSpec as P

epsilon = 1e-05
MESH = pl.DeviceIdType.MESH
F32 = jnp.float32
BF16 = jnp.bfloat16
TAIL = 16


def dot(a, b, dims):
    return lax.dot_general(a, b, (dims, ((), ())), preferred_element_type=F32)


def split_rows(row):
    wide = jnp.broadcast_to(row, (TAIL, row.shape[-1]))
    high = wide.astype(BF16).astype(F32)
    at = lax.broadcasted_iota(jnp.int32, wide.shape, 0)
    return jnp.where(at < 8, high, wide - high).astype(BF16)


def joined_row(tail):
    tail = tail.astype(F32)
    return tail[0:1] + tail[8:9]


def as_column(row, lanes):
    return jnp.broadcast_to(row, (lanes, row.shape[-1])).T


def kernel(
    n_pipe, n_dp,
    gains, inputs, cotangent, w_value, w_out,
    gv_out, go_out, gg_out,
    wv_all, wo_all, ga_all, h0_all, cot_all, own_h, vq, xs, xbuf,
    h_all, g_all, g_own, acc_v, acc_o, acc_g, gs_v, gs_o, gs_g,
    w_send, w_recv, in_send, in_recv, x_send, x_recv,
    v_send, v_recv, d_send, d_recv, o_send, o_recv,
):
    me = lax.axis_index("pipe")
    z = lax.axis_index("dp")
    layers = n_pipe
    width = wv_all.shape[1]
    full = width * n_pipe
    rank = wv_all.shape[2]
    tokens = own_h.shape[1]

    def plane_peer(k):
        return lax.rem(me + k, n_pipe)

    def line_peer(k):
        return lax.rem(z + k, n_dp)

    barrier = pltpu.get_barrier_semaphore()
    for k in range(1, n_pipe):
        pl.semaphore_signal(barrier, inc=1, device_id=(plane_peer(k), z), device_id_type=MESH)
    for k in range(1, n_dp):
        pl.semaphore_signal(barrier, inc=1, device_id=(me, line_peer(k)), device_id_type=MESH)
    pl.semaphore_wait(barrier, n_pipe + n_dp - 2)

    def columns(owner):
        return pl.ds(pl.multiple_of(owner * width, width), width)

    def remote(src, dst, send, recv, to):
        return pltpu.make_async_remote_copy(
            src_ref=src, dst_ref=dst, send_sem=send, recv_sem=recv, device_id=to, device_id_type=MESH
        )

    def wait_local(dst, sem):
        pltpu.make_async_copy(dst, dst, sem).wait()

    pltpu.make_async_copy(inputs.at[:, :, columns(me)], h0_all.at[z], in_recv.at[0, 0]).start()
    pltpu.make_async_copy(cotangent.at[:, :, columns(me)], cot_all.at[z], in_recv.at[1, 0]).start()
    pltpu.make_async_copy(gains.at[:, columns(me)], ga_all.at[me], w_recv.at[0, me]).start()
    pltpu.make_async_copy(w_value.at[columns(me), :], wv_all.at[me], w_recv.at[1, me]).start()
    pltpu.make_async_copy(w_out.at[:, columns(me)], wo_all.at[me], w_recv.at[2, me]).start()

    def weight_copies(k):
        d = plane_peer(k)
        return (
            remote(gains.at[:, columns(d)], ga_all.at[me], w_send.at[0, k], w_recv.at[0, me], (d, z)),
            remote(w_value.at[columns(d), :], wv_all.at[me], w_send.at[1, k], w_recv.at[1, me], (d, z)),
            remote(w_out.at[:, columns(d)], wo_all.at[me], w_send.at[2, k], w_recv.at[2, me], (d, z)),
        )

    def input_copies(k):
        d = line_peer(k)
        return (
            remote(inputs.at[:, :, columns(me)], h0_all.at[z], in_send.at[0, k], in_recv.at[0, k], (me, d)),
            remote(cotangent.at[:, :, columns(me)], cot_all.at[z], in_send.at[1, k], in_recv.at[1, k], (me, d)),
        )

    def line_copies(buf, send, recv, s):
        return [
            remote(buf.at[s, z], buf.at[s, z], send.at[s, k], recv.at[s, k], (me, line_peer(k)))
            for k in range(1, n_dp)
        ]

    def exchange_copies(slot, rows):
        return [
            remote(
                xbuf.at[slot, 0, pl.ds(0, rows)], xbuf.at[slot, k, pl.ds(0, rows)],
                x_send.at[slot, k], x_recv.at[slot, k], (plane_peer(k), z),
            )
            for k in range(1, n_pipe)
        ]

    for k in range(1, n_pipe):
        for copy in weight_copies(k):
            copy.start()
    for k in range(1, n_dp):
        for copy in input_copies(k):
            copy.start()

    wait_local(h0_all.at[z], in_recv.at[0, 0])
    wait_local(cot_all.at[z], in_recv.at[1, 0])
    own_h[0] = h0_all[z].reshape(tokens, width)
    g_own[...] = cot_all[z].reshape(tokens, width).astype(F32)

    def forward(s, carry):
        slot = lax.rem(s, 2)
        wait_local(ga_all.at[s], w_recv.at[0, s])
        wait_local(wv_all.at[s], w_recv.at[1, s])
        floats = own_h[s].astype(F32)
        scaled = (floats * ga_all[s, 0:1, :]).astype(BF16)
        part = dot(scaled, wv_all[s], ((1,), (0,)))
        squares = dot(jnp.ones((8, width), BF16), (floats * floats).astype(BF16), ((1,), (1,)))
        xbuf[slot, 0, 0:tokens, :] = part.astype(BF16)
        xbuf[slot, 0, tokens:, :] = split_rows(squares[0:1])
        copies = exchange_copies(slot, tokens + TAIL)
        for copy in copies:
            copy.start()
        wait_local(wo_all.at[s], w_recv.at[2, s])
        row = joined_row(xbuf[slot, 0, tokens:, :])
        total = part
        for k, copy in enumerate(copies, 1):
            copy.wait_recv()
            total = total + xbuf[slot, k, 0:tokens, :].astype(F32)
            row = row + joined_row(xbuf[slot, k, tokens:, :])
        scale = lax.rsqrt(row * (1.0 / full) + epsilon)
        values = (total * as_column(scale, rank)).astype(BF16)
        vq[s, z, 0:tokens, :] = values
        vq[s, z, tokens:, :] = split_rows(scale)
        for copy in line_copies(vq, v_send, v_recv, s):
            copy.start()
        own_h[s + 1] = (floats + dot(values, wo_all[s], ((1,), (0,)))).astype(BF16)
        for copy in copies:
            copy.wait_send()
        return carry

    lax.fori_loop(0, layers, forward, 0)

    def fill_all():
        for k in range(1, n_dp):
            for copy in input_copies(k):
                copy.wait()

        def arrive(s, carry):
            for copy in line_copies(vq, v_send, v_recv, s):
                copy.wait()
            return carry

        lax.fori_loop(0, layers, arrive, 0)

        def replica(r, carry):
            g_all[r] = cot_all[r].reshape(tokens, width).astype(F32)
            h_all[r] = h0_all[r].reshape(tokens, width).astype(F32)

            def add(s, inner):
                h_all[r] += dot(vq[s, r, 0:tokens, :], wo_all[s], ((1,), (0,)))
                return inner

            lax.fori_loop(0, layers, add, 0)
            return carry

        lax.fori_loop(0, n_dp, replica, 0)

    def gradients(s):
        for copy in line_copies(xs, d_send, d_recv, s):
            copy.wait()
        acc_v[...] = jnp.zeros_like(acc_v)
        acc_o[...] = jnp.zeros_like(acc_o)
        acc_g[...] = jnp.zeros_like(acc_g)

        def replica(r, carry):
            gain = ga_all[s, 0:1, :]
            values = vq[s, r, 0:tokens, :]
            scale = as_column(joined_row(vq[s, r, tokens:, :]), rank)
            scaled_dv = xs[s, r]
            floats = h_all[r] - dot(values, wo_all[s], ((1,), (0,)))
            h_all[r] = floats
            upper = g_all[r]
            acc_o[...] += dot(values, upper.astype(BF16), ((0,), (0,)))
            acc_v[...] += dot((floats * gain).astype(BF16), scaled_dv, ((0,), (0,)))
            du = dot(scaled_dv, wv_all[s], ((1,), (1,)))
            acc_g[0:1, :] += jnp.sum(du * floats, axis=0, keepdims=True)
            weigh = jnp.sum(scaled_dv.astype(F32) * values.astype(F32) * scale, axis=1, keepdims=True)
            g_all[r] = upper + (du * gain - floats * (weigh * (1.0 / full)))
            return carry

        lax.fori_loop(0, n_dp, replica, 0)
        gs_v[s] = acc_v[...].astype(BF16)
        gs_o[s] = acc_o[...].astype(BF16)
        gs_g[s] = acc_g[...]

    def send_out(s):
        @pl.when(s == me)
        def _():
            pltpu.make_async_copy(gs_v.at[s], gv_out.at[me], o_recv.at[0, me]).start()
            pltpu.make_async_copy(gs_o.at[s], go_out.at[:, columns(me)], o_recv.at[1, me]).start()
            pltpu.make_async_copy(gs_g.at[s], gg_out.at[me], o_recv.at[2, me]).start()

        @pl.when(s != me)
        def _():
            remote(gs_v.at[s], gv_out.at[me], o_send.at[0, s], o_recv.at[0, me], (s, z)).start()
            remote(gs_o.at[s], go_out.at[:, columns(me)], o_send.at[1, s], o_recv.at[1, me], (s, z)).start()
            remote(gs_g.at[s], gg_out.at[me], o_send.at[2, s], o_recv.at[2, me], (s, z)).start()

    def backward(i, carry):
        s = layers - 1 - i
        slot = lax.rem(layers + i, 2)
        upper = g_own[...]
        part = dot(upper.astype(BF16), wo_all[s], ((1,), (1,)))
        xbuf[slot, 0, 0:tokens, :] = part.astype(BF16)
        copies = exchange_copies(slot, tokens)
        for copy in copies:
            copy.start()

        @pl.when(i == 0)
        def _():
            fill_all()

        @pl.when(i > 0)
        def _():
            gradients(s + 1)

        total = part
        for k, copy in enumerate(copies, 1):
            copy.wait_recv()
            total = total + xbuf[slot, k, 0:tokens, :].astype(F32)
        scale = as_column(joined_row(vq[s, z, tokens:, :]), rank)
        scaled_dv = (total * scale).astype(BF16)
        xs[s, z] = scaled_dv
        for copy in line_copies(xs, d_send, d_recv, s):
            copy.start()
        values = vq[s, z, 0:tokens, :].astype(F32)
        weigh = jnp.sum(scaled_dv.astype(F32) * values * scale, axis=1, keepdims=True)
        du = dot(scaled_dv, wv_all[s], ((1,), (1,)))
        floats = own_h[s].astype(F32)
        g_own[...] = upper + (du * ga_all[s, 0:1, :] - floats * (weigh * (1.0 / full)))
        for copy in copies:
            copy.wait_send()
        return carry

    lax.fori_loop(0, layers, backward, 0)
    def early(k):
        return ((k == n_pipe // 2) | (k == n_pipe // 4) | (k == 0)) & (lax.rem(me + k, n_pipe) != 0)

    def send_early(k, carry):
        @pl.when(early(k))
        def _():
            send_out(lax.rem(me + k, n_pipe))

        return carry

    def send_late(k, carry):
        @pl.when(jnp.logical_not(early(k)))
        def _():
            send_out(lax.rem(me + k, n_pipe))

        return carry

    lax.fori_loop(0, n_pipe, send_early, 0)
    gradients(0)
    lax.fori_loop(0, n_pipe, send_late, 0)

    for k in range(1, n_pipe):
        for copy in weight_copies(k):
            copy.wait_send()

    def finish(s, carry):
        wait_local(gv_out.at[s], o_recv.at[0, s])
        wait_local(go_out.at[:, columns(s)], o_recv.at[1, s])
        wait_local(gg_out.at[s], o_recv.at[2, s])

        @pl.when(s != me)
        def _():
            remote(gs_v.at[s], gv_out.at[me], o_send.at[0, s], o_recv.at[0, me], (s, z)).wait_send()
            remote(gs_o.at[s], go_out.at[:, columns(me)], o_send.at[1, s], o_recv.at[1, me], (s, z)).wait_send()
            remote(gs_g.at[s], gg_out.at[me], o_send.at[2, s], o_recv.at[2, me], (s, z)).wait_send()

        return carry

    lax.fori_loop(0, n_pipe, finish, 0)


def per_device(n_pipe, n_dp, inputs, cotangent, gains, w_value, w_out):
    batches, rows, full = inputs.shape
    rank = w_value.shape[-1]
    width = full // n_pipe
    tokens = batches * rows
    layers = n_pipe
    any_spec = pl.BlockSpec(memory_space=pl.ANY)
    dma = pltpu.SemaphoreType.DMA
    gv, go, gg = pl.pallas_call(
        functools.partial(kernel, n_pipe, n_dp),
        out_shape=(
            jax.ShapeDtypeStruct((n_pipe, width, rank), BF16),
            jax.ShapeDtypeStruct((rank, full), BF16),
            jax.ShapeDtypeStruct((n_pipe, 1, width), F32),
        ),
        in_specs=[any_spec] * 5,
        out_specs=(any_spec,) * 3,
        scratch_shapes=[
            pltpu.VMEM((layers, width, rank), BF16),
            pltpu.VMEM((layers, rank, width), BF16),
            pltpu.VMEM((layers, 1, width), F32),
            pltpu.VMEM((n_dp, batches, rows, width), BF16),
            pltpu.VMEM((n_dp, batches, rows, width), BF16),
            pltpu.VMEM((layers + 1, tokens, width), BF16),
            pltpu.VMEM((layers, n_dp, tokens + TAIL, rank), BF16),
            pltpu.VMEM((layers, n_dp, tokens, rank), BF16),
            pltpu.VMEM((2, n_pipe, tokens + TAIL, rank), BF16),
            pltpu.VMEM((n_dp, tokens, width), F32),
            pltpu.VMEM((n_dp, tokens, width), F32),
            pltpu.VMEM((tokens, width), F32),
            pltpu.VMEM((width, rank), F32),
            pltpu.VMEM((rank, width), F32),
            pltpu.VMEM((1, width), F32),
            pltpu.VMEM((layers, width, rank), BF16),
            pltpu.VMEM((layers, rank, width), BF16),
            pltpu.VMEM((layers, 1, width), F32),
            dma((3, n_pipe)), dma((3, n_pipe)),
            dma((2, n_dp)), dma((2, n_dp)),
            dma((2, n_pipe)), dma((2, n_pipe)),
            dma((layers, n_dp)), dma((layers, n_dp)),
            dma((layers, n_dp)), dma((layers, n_dp)),
            dma((3, n_pipe)), dma((3, n_pipe)),
        ],
        compiler_params=pltpu.CompilerParams(
            collective_id=0, has_side_effects=True, vmem_limit_bytes=56 * 1024 * 1024
        ),
        cost_estimate=pl.CostEstimate(
            flops=40 * n_dp * tokens * full * rank, bytes_accessed=16 * full * rank, transcendentals=0
        ),
    )(gains, inputs, cotangent, w_value[0], w_out[0])
    return (
        gv.reshape(1, full, rank).astype(F32),
        go[None].astype(F32),
        gg.reshape(1, full),
    )


def solution(mesh):
    placed = (
        P(None, "dp", None),
        P(None, "dp", None),
        P("pipe", None),
        P("pipe", None, None),
        P("pipe", None, None),
    )
    return jax.shard_map(
        functools.partial(per_device, mesh.shape["pipe"], mesh.shape["dp"]),
        mesh=mesh,
        in_specs=placed,
        out_specs=(P("pipe", None, None), P("pipe", None, None), P("pipe", None)),
        check_vma=False,
    )
```
